32 devices in a mesh: groups: 2 (over x), tensor: 16 (over z, y, core).
Axes of the slice: x: 2, y: 2, z: 4, core: 2. Of those that a mesh axis runs over, the one named last changes fastest.
Arguments:
- hidden_in: bfloat16 [256, 8192], P('groups', 'tensor'), parts along dimension 0, may hold values from -6 to 6
- norm_gain: bfloat16 [8192], replicated, may hold values from 0.099609375 to 1.8984375
- query_base_matrix: bfloat16 [8192, 8192], P(None, 'tensor'), may hold values from -0.0625 to 0.0625
- kv_weight: bfloat16 [8192, 2048], P('tensor'), may hold values from -0.0625 to 0.0625
- out_weight: bfloat16 [8192, 8192], P('tensor'), may hold values from -0.09375 to 0.09375
- query_down: bfloat16 [16, 8192, 64], P('tensor'), may hold values from -0.0625 to 0.0625
- query_up_factor: bfloat16 [16, 64, 8192], P('tensor'), may hold values from -0.75 to 0.75
- output_down: bfloat16 [16, 8192, 64], P('tensor'), may hold values from -0.0625 to 0.0625
- output_up_factor: bfloat16 [16, 64, 8192], P('tensor'), may hold values from -0.75 to 0.75
- variant_ids: int32 [256, 1], P('groups'), parts along dimension 0, may hold values from 0 to 15
- cache_lengths: int32 [256], P('groups'), parts along dimension 0, may hold values from 1 to 16, 1280 in all
- kv_cache: bfloat16 [16, 256, 16, 256], P('tensor', 'groups'), parts along dimension 1, as said below
Outputs:
- projected: bfloat16 [256, 8192], P('groups', 'tensor'), parts along dimension 0
The draws below stay inside these ranges and needn't reach their ends.
There are 2 independent parts, one for each index of `groups`. The reference program is written for one: setup_inputs(seed, part) draws one part's arguments, and reference() takes and returns one part's arrays. A program takes and returns all parts, laid end to end along the dimension named above; an argument that names none is the same for every part. Nothing has to cross between parts.
Inputs may be any that keep to these rules, and one draw needn't show every extreme that they name: `variant_ids`: every one of the 16 variants is named by at least one row. `kv_cache`: the 2 copies of one key-value head are identical: copy c equals copy c2 whenever c // 2 == c2 // 2.
All inputs are finite; a program needn't handle non-finite values.
Results may differ from the reference program's by a relative error of at most 0.012.
The reference program's roundings to bfloat16 on the way count: a program that leaves them out, or rounds other values in their place, can miss the bound.
Values may be sent and summed in bfloat16 or wider, within the bound.
A program may use at most 128 MiB of HBM per device.

```python
import math
import jax
import jax.numpy as jnp
import numpy as np
from jax import lax

D = 8192
H = 64
KVH = 8
HD = 128
RANK = 64
ROWS = 128
CACHE = 16
VARIANTS = 16
COPIES = 16


def draw_kv_cache(key, part):
    key = jax.random.fold_in(key, 11)
    shape = (KVH, ROWS, CACHE, 2 * HD)
    base_product = jax.random.normal(key, shape, jnp.float32)
    return jnp.repeat(base_product, COPIES // KVH, axis=0).astype(jnp.bfloat16)


def with_spikes(entries, key, source, target, parts, factor):
    def block_of(position):
        return (jnp.arange(entries.shape[position]) // (entries.shape[position] // parts)).reshape((-1,) + (1,) * (entries.ndim - 1 - position))

    one_side = jax.random.permutation(key, parts)[block_of(target)]
    far = (block_of(target) + parts // 2) % parts
    return jnp.where((block_of(source) == one_side) | (block_of(source) == far), factor * entries, entries)


def shard_levels(key, dims, split, low, top_value):
    loudness, own = 1.0, jax.random.fold_in(key, 6)
    for position, parts in split:
        heights = jnp.exp(jax.random.uniform(jax.random.fold_in(own, position), (parts,), jnp.float32, low / len(split), top_value / len(split)))
        loudness = loudness * jnp.repeat(heights, dims[position] // parts).reshape([-1 if axis == position else 1 for axis in range(len(dims))])
    return loudness


def distinct(stream_key, rows, count, top, lift):
    order = jax.random.permutation(jax.random.fold_in(stream_key, 1), count)
    favour = order
    for power in range(3):
        favour = favour * favour // count
    favour = favour * lift // count
    tickets = jax.random.randint(jax.random.fold_in(stream_key, 2), (rows, count), 0, 4096) + favour
    holders = jax.random.permutation(jax.random.fold_in(stream_key, 3), rows)[jnp.arange(count) % rows]
    tickets = jnp.where(jnp.arange(rows)[:, None] == holders[None, :], 1 << 14, tickets)
    score = tickets * count + jnp.arange(count)
    return lax.top_k(score.astype(jnp.int32), top)[1].astype(jnp.int32)


def split_up(count, total, bound, lean):
    weights = [(1 << 20) // math.isqrt(rank ** lean) + 1 for rank in range(2, count + 1)]
    rest, counts = total - bound - (count - 1), [1] * (count - 1)
    while rest > 0:
        free = [i for i in range(count - 1) if counts[i] < bound]
        whole, remaining = sum([weights[i] for i in free]), rest
        for i in free:
            more = min(bound - counts[i], max(1, remaining * weights[i] // whole), rest)
            counts[i] = counts[i] + more
            rest = rest - more
    return np.array([bound] + counts)


def uneven(rng, number_of, total, reach, slope):
    if number_of == 2:
        one = jax.random.randint(rng, (), max(1, total - reach), min(reach, total - 1) + 1)
        return jnp.stack([one, total - one])
    lengths = jnp.asarray(split_up(number_of, total, reach, slope), jnp.int32)
    couples = (number_of - 1) // 2
    source_of, sink = lengths[1:1 + 2 * couples:2], lengths[2:2 + 2 * couples:2]
    room = jnp.minimum(source_of - 1, reach - sink)
    shifted = jax.random.randint(jax.random.fold_in(rng, 1), (couples,), 0, 1 << 20) % (room + 1)
    lengths = lengths.at[1:1 + 2 * couples:2].set(source_of - shifted).at[2:2 + 2 * couples:2].set(sink + shifted)
    return lengths[jax.random.permutation(jax.random.fold_in(rng, 2), number_of)]


def scatter_about(key, dims, scale, limit, split=(), kind=jnp.bfloat16):
    level = shard_levels(key, dims, split, -0.22, 0.18) if split else 1.0
    entries = jax.random.normal(key, dims, jnp.float32) * scale * level
    return jnp.minimum(jnp.maximum(entries, -limit), limit).astype(kind)


def gaussian_with(stream_key, extent, scale, bound, pieces, heavy, kind=jnp.bfloat16):
    array = scale * jax.random.normal(stream_key, extent, jnp.float32)
    if pieces:
        array = array * shard_levels(stream_key, extent, pieces, -0.22, 0.18)
    return jnp.clip(with_spikes(array, jax.random.fold_in(stream_key, 3), *heavy), -bound, bound).astype(kind)


def setup_inputs(seed: int = 0, part: int = 0) -> dict:
    seeds = jax.random.split(jax.random.key(seed), 13)
    own_keys = jax.random.split(jax.random.fold_in(seeds[12], part), 13)
    return {
        "hidden_in": scatter_about(own_keys[0], (ROWS, D), 1.0, 6.0, ((1, 16),)),
        "norm_gain": jnp.clip(1.0 + 0.18 * jax.random.normal(seeds[1], (D,), jnp.float32), 0.099609375, 1.8984375).astype(jnp.bfloat16),
        "query_base_matrix": scatter_about(seeds[2], (D, H * HD), D ** -0.5, 0.0625, ((1, 16),)),
        "kv_weight": scatter_about(seeds[3], (D, KVH * 2 * HD), D ** -0.5, 0.0625, ((0, 16),)),
        "out_weight": gaussian_with(seeds[4], (H * HD, D), (H * HD) ** -0.5, 0.09375, ((0, 16),), (0, 1, 16, 2.0)),
        "query_down": scatter_about(seeds[5], (VARIANTS, D, RANK), D ** -0.5, 0.0625, ((0, 16),)),
        "query_up_factor": scatter_about(seeds[6], (VARIANTS, RANK, H * HD), RANK ** -0.5, 0.75, ((0, 16),)),
        "output_down": scatter_about(seeds[7], (VARIANTS, H * HD, RANK), (H * HD) ** -0.5, 0.0625, ((0, 16),)),
        "output_up_factor": scatter_about(seeds[8], (VARIANTS, RANK, D), RANK ** -0.5, 0.75, ((0, 16),)),
        "variant_ids": distinct(own_keys[9], ROWS, VARIANTS, 1, 1024),
        "cache_lengths": uneven(own_keys[10], ROWS, ROWS * CACHE * 5 // 8, CACHE, 1).astype(jnp.int32),
        "kv_cache": draw_kv_cache(jax.random.fold_in(jax.random.fold_in(seeds[12], part), 71), part),
    }


adapter_scale = 2.0

def gather_variant_rows(left, tables, picked_variants):
    catalog = jnp.arange(tables.shape[0], dtype=jnp.int32)

    def step(total, item):
        index, table = item
        term = jnp.dot(left, table, preferred_element_type=jnp.float32)
        return (total + jnp.where((picked_variants == index)[:, None], term, jnp.float32(0.0)), None)
    init = jnp.zeros((left.shape[0], tables.shape[2]), jnp.float32)
    return lax.scan(step, init, (catalog, tables))[0]

def reference(hidden_in, norm_gain, query_base_matrix, kv_weight, out_weight, query_down, query_up_factor, output_down, output_up_factor, variant_ids, cache_lengths, kv_cache):
    wide = hidden_in.astype(jnp.float32)
    normalized_input = (wide * lax.rsqrt(lax.optimization_barrier(jnp.mean(wide * wide, axis=1, keepdims=True)) + 1e-06) * norm_gain.astype(jnp.float32)).astype(jnp.bfloat16)
    picked_variants = variant_ids[:, 0]
    query_factor_rows = gather_variant_rows(normalized_input, query_down, picked_variants).astype(jnp.bfloat16)
    query_vectors = (jnp.dot(normalized_input, query_base_matrix, preferred_element_type=jnp.float32) + adapter_scale * gather_variant_rows(query_factor_rows, query_up_factor, picked_variants)).astype(jnp.bfloat16)
    fresh = jnp.dot(normalized_input, kv_weight, preferred_element_type=jnp.float32).astype(jnp.bfloat16)
    per_copy = H // COPIES
    group = H // KVH
    positions = jnp.arange(CACHE, dtype=jnp.int32)
    live = positions[None, :] < cache_lengths[:, None]
    scale = 1.0 / HD ** 0.5

    def one_head(head):
        query_head = lax.dynamic_slice_in_dim(query_vectors, head * HD, HD, 1).astype(jnp.float32)
        stored = lax.dynamic_index_in_dim(kv_cache, (head // per_copy).astype(jnp.int32), 0, keepdims=False).astype(jnp.float32)
        fresh_head = lax.dynamic_slice_in_dim(fresh, (head // group * 2 * HD).astype(jnp.int32), 2 * HD, 1).astype(jnp.float32)
        keys = stored[:, :, :HD]
        values = stored[:, :, HD:]
        scores = jnp.einsum('rd,rld->rl', query_head, keys) * scale
        own = lax.optimization_barrier(jnp.sum(query_head * fresh_head[:, :HD], axis=1)) * scale
        scores = jnp.where(live, scores, -jnp.inf)
        top = jnp.maximum(lax.optimization_barrier(jnp.max(scores, axis=1)), own)
        expo = jnp.exp(scores - top[:, None])
        own_expo = jnp.exp(own - top)
        total = lax.optimization_barrier(jnp.sum(expo, axis=1)) + own_expo
        weights = (expo / total[:, None]).astype(jnp.bfloat16).astype(jnp.float32)
        own_weight = (own_expo / total).astype(jnp.bfloat16).astype(jnp.float32)
        result = jnp.einsum('rl,rld->rd', weights, values) + own_weight[:, None] * fresh_head[:, HD:]
        return result.astype(jnp.bfloat16)
    heads = lax.map(one_head, jnp.arange(H, dtype=jnp.int32))
    attended = jnp.transpose(heads, (1, 0, 2)).reshape(ROWS, H * HD)
    output_factor_rows = gather_variant_rows(attended, output_down, picked_variants).astype(jnp.bfloat16)
    base_product = jnp.dot(attended, out_weight, preferred_element_type=jnp.float32)
    return (base_product + adapter_scale * gather_variant_rows(output_factor_rows, output_up_factor, picked_variants)).astype(jnp.bfloat16)
```

```python
import functools

import jax
import jax.numpy as jnp
from jax import lax
from jax.experimental import pallas as pl
from jax.experimental.pallas import tpu as pltpu
from jax.sharding import PartitionSpec as P

H = 64
KVH = 8
HD = 128
MESH = pl.DeviceIdType.MESH
F32 = jnp.float32
BF16 = jnp.bfloat16

adapter_scale = 2.0


def chip_of(p, chips):
    if chips == 8:
        return 2 * p + lax.div(p, 4) * (15 - 4 * p)
    return p


def place_of(c, chips):
    if chips == 8:
        z = lax.div(c, 2)
        return z + lax.rem(c, 2) * (7 - 2 * z)
    return c


class Ring:
    def __init__(self, n):
        self.n = n
        self.chips = n // 2
        self.long = self.chips // 2
        self.short = self.chips - 1 - self.long
        self.me = lax.axis_index("tensor")
        self.core = lax.rem(self.me, 2)
        self.place = place_of(lax.div(self.me, 2), self.chips)
        self.sign = 1 - 2 * self.core
        self.right = self.at(1)
        self.left = self.at(-1)
        self.mate = self.chip(0) * 2 + 1 - self.core

    def chip(self, off):
        return chip_of(
            lax.rem(self.place + off * self.sign + 2 * self.chips, self.chips), self.chips
        )

    def at(self, off, other=False):
        core = 1 - self.core if other else self.core
        return self.chip(off) * 2 + core

    def barrier(self):
        sem = pltpu.get_barrier_semaphore()
        for device in (self.right, self.left, self.mate):
            pl.semaphore_signal(sem, inc=1, device_id={"tensor": device}, device_id_type=MESH)
        pl.semaphore_wait(sem, 3)

    def copy(self, src, dst, ssem, rsem, device):
        return pltpu.make_async_remote_copy(
            src_ref=src,
            dst_ref=dst,
            send_sem=ssem,
            recv_sem=rsem,
            device_id={"tensor": device},
            device_id_type=MESH,
        )


def gather_sems(n):
    return [pltpu.SemaphoreType.DMA((n - 1,)), pltpu.SemaphoreType.DMA((n - 1,))]


def gather_blocks(ring, blocks, ssem, rsem, between, on_block):
    long, short, chips = ring.long, ring.short, ring.chips
    sent = []

    def send(slot, index, device):
        one = ring.copy(blocks.at[slot], blocks.at[slot], ssem.at[index], rsem.at[index], device)
        one.start()
        sent.append(one)

    def arrived(slot, index):
        ring.copy(
            blocks.at[slot], blocks.at[slot], ssem.at[index], rsem.at[index], ring.mate
        ).wait_recv()

    hand = chips - 1
    send(ring.me, 0, ring.right)
    send(ring.me, long, ring.left)
    send(ring.me, hand, ring.mate)
    between()
    arrived(ring.mate, hand)
    on_block(ring.mate)
    for j in range(1, long + 1):
        slot = ring.at(-j)
        arrived(slot, j - 1)
        if j < long:
            send(slot, j, ring.right)
        send(slot, hand + j, ring.mate)
        if j <= short:
            other = ring.at(j)
            arrived(other, long + j - 1)
            if j < short:
                send(other, long + j, ring.left)
            send(other, hand + long + j, ring.mate)
        on_block(slot)
        if j <= short:
            on_block(other)
        slot = ring.at(j, True)
        arrived(slot, hand + j)
        on_block(slot)
        if j <= short:
            slot = ring.at(-j, True)
            arrived(slot, hand + long + j)
            on_block(slot)
    for one in sent:
        one.wait_send()


def scatter_scratch(n, rows, width):
    chips = n // 2
    return [
        pltpu.VMEM((chips, rows, width), BF16),
        pltpu.VMEM((chips, rows, width), BF16),
        pltpu.VMEM((chips - 1, rows, width), BF16),
        pltpu.VMEM((chips - 1, rows, width), BF16),
        pltpu.SemaphoreType.DMA((n - 1,)),
        pltpu.SemaphoreType.DMA((n - 1,)),
    ]


def scatter_sum(ring, partial, hand_out, hand_in, going, coming, ssem, rsem):
    long, short, chips = ring.long, ring.short, ring.chips
    order = []
    for j in range(long, 0, -1):
        order.append(j)
        if j > 1:
            order.append(1 - j)
    order = [o for o in order if -short <= o <= long] + [0]
    sent = []
    base = chips - 1
    for i, o in enumerate(order):
        hand_out[i] = partial(ring.chip(-o), 1 - ring.core).astype(BF16)
        one = ring.copy(
            hand_out.at[i], hand_in.at[i], ssem.at[base + i], rsem.at[base + i], ring.mate
        )
        one.start()
        sent.append(one)

    def arrived(buf, index, sem):
        ring.copy(buf.at[index], buf.at[index], ssem.at[sem], rsem.at[sem], ring.mate).wait_recv()
        return buf[index].astype(F32)

    for i, o in enumerate(order):
        value = partial(ring.chip(o), ring.core)
        value = value + arrived(hand_in, i, base + i)
        if o > 0:
            step = long - o
            first, device, slot = step == 0, ring.right, step
        elif o < 0:
            step = short + o
            first, device, slot = step == 0, ring.left, long + step
        else:
            value = value + arrived(coming, long - 1, long - 1)
            if short:
                value = value + arrived(coming, long + short - 1, long + short - 1)
            break
        if not first:
            value = value + arrived(coming, slot - 1, slot - 1)
        going[slot] = value.astype(BF16)
        one = ring.copy(going.at[slot], coming.at[slot], ssem.at[slot], rsem.at[slot], device)
        one.start()
        sent.append(one)
    for one in sent:
        one.wait_send()
    return value


def columns(index, width):
    return pl.ds(pl.multiple_of(index * width, width), width)


def dot(a, b):
    return jnp.dot(a, b, preferred_element_type=F32)


def dot_t(a, b):
    return lax.dot_general(a, b, (((1,), (1,)), ((), ())), preferred_element_type=F32)


def first_kernel(
    n,
    hidden,
    gain,
    ids,
    wq_hbm,
    kvw_hbm,
    down_hbm,
    up_hbm,
    query,
    pair,
    blocks,
    wq,
    kvw,
    down,
    up,
    normed,
    total,
    factor,
    halves,
    wsem,
    gs,
    gr,
    fsem,
    *scatter,
):
    ring = Ring(n)
    loads = [
        pltpu.make_async_copy(src, dst, wsem.at[i])
        for i, (src, dst) in enumerate(
            ((wq_hbm, wq), (down_hbm, down), (kvw_hbm, kvw), (up_hbm, up))
        )
    ]
    for load in loads:
        load.start()
    rows, width = hidden.shape
    blocks[ring.me] = hidden[...]
    ring.barrier()

    def add_square(x):
        wide = x.astype(F32)
        total[...] += jnp.sum(wide * wide, axis=1, keepdims=True)

    def between():
        total[...] = jnp.zeros_like(total)
        add_square(hidden[...])
        query_sum[...] = jnp.zeros_like(query_sum)
        factor[...] = jnp.zeros_like(factor)

    query_sum = scatter[-1]
    scatter = scatter[:-1]
    gather_blocks(ring, blocks, gs, gr, between, lambda slot: add_square(blocks[slot]))
    inverse = lax.rsqrt(total[...] * (1.0 / (n * width)) + 1e-06)
    for load in loads:
        load.wait()

    def project(t, carry):
        part = columns(t, width)
        x = (blocks[t].astype(F32) * inverse * gain[:, part].astype(F32)).astype(BF16)
        normed[t] = x
        query_sum[...] += dot(x, wq[part, :])
        factor[...] += dot_t(x, down[:, part])
        return carry

    lax.fori_loop(0, n, project, 0)
    masked = jnp.where(ids[...] == ring.me, factor[...], 0.0).astype(BF16)
    own = normed[ring.me]
    devices_a_head = n // KVH

    def partial(chip, core):
        head = lax.div(chip * 2, devices_a_head)
        delta = dot(masked, up[:, columns(chip * 2 + core, width)])
        fresh = dot(own, kvw[:, columns(head * 2 + core, HD)])
        return jnp.concatenate([delta, fresh], axis=1)

    value = scatter_sum(ring, partial, *scatter)
    halves[ring.core] = value[:, width:].astype(BF16)
    swap = ring.copy(
        halves.at[ring.core], halves.at[ring.core], fsem.at[0], fsem.at[1], ring.mate
    )
    swap.start()
    query[...] = (query_sum[...] + adapter_scale * value[:, :width]).astype(BF16)
    swap.wait_send()
    other = halves.at[1 - ring.core]
    ring.copy(other, other, fsem.at[0], fsem.at[1], ring.mate).wait_recv()
    pair[...] = halves[...]


def second_kernel(
    n,
    attended,
    ids,
    wo_hbm,
    down_hbm,
    up_hbm,
    out,
    blocks,
    wo,
    down,
    up,
    base,
    factor,
    wsem,
    gs,
    gr,
    *scatter,
):
    ring = Ring(n)
    loads = [
        pltpu.make_async_copy(src, dst, wsem.at[i])
        for i, (src, dst) in enumerate(((wo_hbm, wo), (down_hbm, down), (up_hbm, up)))
    ]
    for load in loads:
        load.start()
    rows, width = attended.shape
    blocks[ring.me] = attended[...]
    ring.barrier()

    def on_block(slot):
        factor[...] += dot_t(blocks[slot], down[:, columns(slot, width)])

    def between():
        for load in loads:
            load.wait()

        def one(t, carry):
            base[t] = dot(attended[...], wo[:, columns(t, width)])
            return carry

        lax.fori_loop(0, n, one, 0)
        factor[...] = dot_t(attended[...], down[:, columns(ring.me, width)])

    gather_blocks(ring, blocks, gs, gr, between, on_block)
    masked = jnp.where(ids[...] == ring.me, factor[...], 0.0).astype(BF16)

    def partial(chip, core):
        t = chip * 2 + core
        return base[t] + adapter_scale * dot(masked, up[:, columns(t, width)])

    out[...] = scatter_sum(ring, partial, *scatter).astype(BF16)


VM = pl.BlockSpec(memory_space=pltpu.VMEM)
ANY = pl.BlockSpec(memory_space=pl.ANY)


def body(
    hidden_in,
    norm_gain,
    query_base_matrix,
    kv_weight,
    out_weight,
    query_down,
    query_up_factor,
    output_down,
    output_up_factor,
    variant_ids,
    cache_lengths,
    kv_cache,
):
    n = lax.axis_size("tensor")
    rows, width = hidden_in.shape
    depth = norm_gain.shape[0]
    rank = query_down.shape[2]
    params = functools.partial(
        pltpu.CompilerParams, has_side_effects=True, vmem_limit_bytes=48 * 1024 * 1024
    )
    query_vectors, pair = pl.pallas_call(
        functools.partial(first_kernel, n),
        out_shape=[
            jax.ShapeDtypeStruct((rows, width), BF16),
            jax.ShapeDtypeStruct((2, rows, HD), BF16),
        ],
        in_specs=[VM] * 3 + [ANY] * 4,
        out_specs=[VM] * 2,
        scratch_shapes=[
            pltpu.VMEM((n, rows, width), BF16),
            pltpu.VMEM(query_base_matrix.shape, BF16),
            pltpu.VMEM(kv_weight.shape, BF16),
            pltpu.VMEM((rank, depth), BF16),
            pltpu.VMEM((rank, depth), BF16),
            pltpu.VMEM((n, rows, width), BF16),
            pltpu.VMEM((rows, 1), F32),
            pltpu.VMEM((rows, rank), F32),
            pltpu.VMEM((2, rows, HD), BF16),
            pltpu.SemaphoreType.DMA((4,)),
            *gather_sems(n),
            pltpu.SemaphoreType.DMA((2,)),
            *scatter_scratch(n, rows, width + HD),
            pltpu.VMEM((rows, width), F32),
        ],
        compiler_params=params(collective_id=0),
        name="gather_project",
    )(
        hidden_in,
        norm_gain[None],
        variant_ids,
        query_base_matrix,
        kv_weight,
        jnp.swapaxes(query_down, 1, 2)[0],
        query_up_factor[0],
    )
    fresh_key, fresh_value = pair[0], pair[1]
    local_heads = width // HD
    query_heads = query_vectors.reshape(rows, local_heads, HD)
    stored = kv_cache[0]
    keys = stored[:, :, :HD]
    values = stored[:, :, HD:]
    scale = 1.0 / HD**0.5
    scores = (
        jnp.einsum("rhd,rld->rhl", query_heads, keys, preferred_element_type=F32) * scale
    )
    own = jnp.einsum("rhd,rd->rh", query_heads, fresh_key, preferred_element_type=F32) * scale
    positions = jnp.arange(stored.shape[1], dtype=jnp.int32)
    live = positions[None, :] < cache_lengths[:, None]
    scores = jnp.where(live[:, None, :], scores, -jnp.inf)
    top = jnp.maximum(jnp.max(scores, axis=2), own)
    expo = jnp.exp(scores - top[:, :, None])
    own_expo = jnp.exp(own - top)
    total = jnp.sum(expo, axis=2) + own_expo
    weights = (expo / total[:, :, None]).astype(BF16)
    own_weight = (own_expo / total).astype(BF16)
    mixed_heads = jnp.einsum("rhl,rld->rhd", weights, values, preferred_element_type=F32)
    mixed_heads = (
        mixed_heads + own_weight.astype(F32)[:, :, None] * fresh_value.astype(F32)[:, None, :]
    )
    attended = mixed_heads.astype(BF16).reshape(rows, local_heads * HD)
    return pl.pallas_call(
        functools.partial(second_kernel, n),
        out_shape=jax.ShapeDtypeStruct((rows, width), BF16),
        in_specs=[VM] * 2 + [ANY] * 3,
        out_specs=VM,
        scratch_shapes=[
            pltpu.VMEM((n, rows, width), BF16),
            pltpu.VMEM(out_weight.shape, BF16),
            pltpu.VMEM((rank, depth), BF16),
            pltpu.VMEM((rank, depth), BF16),
            pltpu.VMEM((n, rows, width), F32),
            pltpu.VMEM((rows, rank), F32),
            pltpu.SemaphoreType.DMA((3,)),
            *gather_sems(n),
            *scatter_scratch(n, rows, width),
        ],
        compiler_params=params(collective_id=1),
        name="gather_output",
    )(
        attended,
        variant_ids,
        out_weight,
        jnp.swapaxes(output_down, 1, 2)[0],
        output_up_factor[0],
    )


def solution(mesh):
    in_specs = (
        P("groups", "tensor"),
        P(),
        P(None, "tensor"),
        P("tensor", None),
        P("tensor", None),
        P("tensor", None, None),
        P("tensor", None, None),
        P("tensor", None, None),
        P("tensor", None, None),
        P("groups", None),
        P("groups"),
        P("tensor", "groups", None, None),
    )
    out_specs = P("groups", "tensor")
    return jax.shard_map(body, mesh=mesh, in_specs=in_specs, out_specs=out_specs, check_vma=False)
```

```python
import functools

import jax
import jax.numpy as jnp
from jax import lax
from jax.experimental import pallas as pl
from jax.experimental.pallas import tpu as pltpu
from jax.sharding import PartitionSpec as P

H = 64
KVH = 8
HD = 128
MESH = pl.DeviceIdType.MESH
F32 = jnp.float32
BF16 = jnp.bfloat16
VMEM_LIMIT = 62 * 1024 * 1024

adapter_scale = 2.0


def chip_of(p, chips):
    if chips == 8:
        return 2 * p + lax.div(p, 4) * (15 - 4 * p)
    return p


def place_of(c, chips):
    if chips == 8:
        z = lax.div(c, 2)
        return z + lax.rem(c, 2) * (7 - 2 * z)
    return c


class Ring:
    def __init__(self, n):
        self.n = n
        self.chips = n // 2
        self.long = self.chips // 2
        self.short = self.chips - 1 - self.long
        self.me = lax.axis_index("tensor")
        self.core = lax.rem(self.me, 2)
        self.place = place_of(lax.div(self.me, 2), self.chips)
        self.sign = 1 - 2 * self.core
        self.right = self.at(1)
        self.left = self.at(-1)
        self.mate = self.chip(0) * 2 + 1 - self.core

    def chip(self, off):
        return chip_of(
            lax.rem(self.place + off * self.sign + 2 * self.chips, self.chips), self.chips
        )

    def at(self, off, other=False):
        core = 1 - self.core if other else self.core
        return self.chip(off) * 2 + core

    def barrier(self):
        sem = pltpu.get_barrier_semaphore()
        for device in (self.right, self.left, self.mate):
            pl.semaphore_signal(sem, inc=1, device_id={"tensor": device}, device_id_type=MESH)
        pl.semaphore_wait(sem, 3)

    def copy(self, src, dst, ssem, rsem, device):
        return pltpu.make_async_remote_copy(
            src_ref=src,
            dst_ref=dst,
            send_sem=ssem,
            recv_sem=rsem,
            device_id={"tensor": device},
            device_id_type=MESH,
        )


def gather_sems(n):
    return [pltpu.SemaphoreType.DMA((2, n - 1)), pltpu.SemaphoreType.DMA((2, n - 1))]


def half(ref, slot, h):
    rows = ref.shape[1] // 2
    return ref.at[slot, pl.ds(h * rows, rows)]


def gather_blocks(ring, blocks, ssem, rsem, filler, on_block):
    long, short, chips = ring.long, ring.short, ring.chips
    sent = []

    def copy(slot, h, index, device):
        ref = half(blocks, slot, h)
        return ring.copy(ref, ref, ssem.at[h, index], rsem.at[h, index], device)

    def send(slot, h, index, device):
        one = copy(slot, h, index, device)
        one.start()
        sent.append(one)

    hand = chips - 1
    for h in range(2):
        send(ring.me, h, 0, ring.right)
        send(ring.me, h, long, ring.left)
    for h in range(2):
        send(ring.me, h, hand, ring.mate)
    filler(0)
    waiting = [(ring.mate, hand)]
    ready = []
    for j in range(1, long + 1):
        slot, other = ring.at(-j), ring.at(j)
        for h in range(2):
            copy(slot, h, j - 1, ring.mate).wait_recv()
            if j < long:
                send(slot, h, j, ring.right)
            send(slot, h, hand + j, ring.mate)
            if j <= short:
                copy(other, h, long + j - 1, ring.mate).wait_recv()
                if j < short:
                    send(other, h, long + j, ring.left)
                send(other, h, hand + long + j, ring.mate)
        filler(j)
        for done, index in waiting:
            for h in range(2):
                copy(done, h, index, ring.mate).wait_recv()
            on_block(done)
        on_block(slot)
        waiting = [(ring.at(j, True), hand + j)]
        if j <= short:
            on_block(other)
            waiting.append((ring.at(-j, True), hand + long + j))
    for done, index in waiting:
        for h in range(2):
            copy(done, h, index, ring.mate).wait_recv()
        on_block(done)
    for one in sent:
        one.wait_send()


def scatter_scratch(n, rows, width):
    chips = n // 2
    return [
        pltpu.VMEM((chips, rows, width), BF16),
        pltpu.VMEM((chips, rows, width), BF16),
        pltpu.VMEM((chips - 1, rows, width), BF16),
        pltpu.VMEM((chips - 1, rows, width), BF16),
        pltpu.VMEM((2, rows, width), F32),
        pltpu.SemaphoreType.DMA((chips,)),
        pltpu.SemaphoreType.DMA((chips,)),
        pltpu.SemaphoreType.DMA((2, chips - 1)),
        pltpu.SemaphoreType.DMA((2, chips - 1)),
    ]


def scatter_sum(ring, partial, filler, hand_out, hand_in, going, coming, held, hs, hr, ssem, rsem):
    long, short, chips = ring.long, ring.short, ring.chips
    rows = going.shape[1] // 2
    steps = []
    for j in range(1, long + 1):
        now = [(2 * j - 2, long - j + 1, j - 1, ring.right, j == 1)]
        if j <= short:
            now.append((2 * j - 1, j - short - 1, long + j - 1, ring.left, j == 1))
        steps.append(now)
    sent = []

    def start(one):
        one.start()
        sent.append(one)

    def hand_copy(i):
        return ring.copy(hand_out.at[i], hand_in.at[i], hs.at[i], hr.at[i], ring.mate)

    def hand_over(i, o):
        hand_out[i] = partial(ring.chip(-o), 1 - ring.core).astype(BF16)
        start(hand_copy(i))

    def hand_overs(j):
        if j < long:
            for i, o, _, _, _ in steps[j]:
                hand_over(i, o)
        elif j == long:
            hand_over(chips - 1, 0)

    def both(i, o):
        value = partial(ring.chip(o), ring.core)
        ring.copy(hand_in.at[i], hand_in.at[i], hs.at[i], hr.at[i], ring.mate).wait_recv()
        return value + hand_in[i].astype(F32)

    def arrived(slot, h):
        ref = half(coming, slot, h)
        ring.copy(ref, ref, ssem.at[h, slot], rsem.at[h, slot], ring.mate).wait_recv()
        return ref[...].astype(F32)

    hand_overs(0)
    hand_overs(1)
    for j, now in enumerate(steps):
        for place, (i, o, slot, device, first) in enumerate(now):
            held[place] = both(i, o)
        for h in range(2):
            part = pl.ds(h * rows, rows)
            for place, (i, o, slot, device, first) in enumerate(now):
                value = held[place, part]
                if not first:
                    value = value + arrived(slot - 1, h)
                going[slot, part] = value.astype(BF16)
                start(
                    ring.copy(
                        half(going, slot, h),
                        half(coming, slot, h),
                        ssem.at[h, slot],
                        rsem.at[h, slot],
                        device,
                    )
                )
        hand_overs(j + 2)
        filler(j)
    if long < 2:
        hand_overs(long)
    held[0] = both(chips - 1, 0)
    for h in range(2):
        part = pl.ds(h * rows, rows)
        value = held[0, part] + arrived(long - 1, h)
        if short:
            value = value + arrived(long + short - 1, h)
        held[0, part] = value
    for one in sent:
        one.wait_send()
    return held[0]


def share(step, steps, count):
    return range(count * step // steps, count * (step + 1) // steps)


def columns(index, width):
    return pl.ds(pl.multiple_of(index * width, width), width)


def dot(a, b):
    return jnp.dot(a, b, preferred_element_type=F32)


def dot_t(a, b):
    return lax.dot_general(a, b, (((1,), (1,)), ((), ())), preferred_element_type=F32)


def first_kernel(
    n,
    hidden,
    gain,
    ids,
    wq_hbm,
    kvw_hbm,
    down_hbm,
    up_hbm,
    query,
    pair,
    blocks,
    wq,
    kvw,
    down,
    up,
    normed,
    total,
    factor,
    halves,
    wsem,
    gs,
    gr,
    fsem,
    *scatter,
):
    ring = Ring(n)
    loads = [
        pltpu.make_async_copy(src, dst, wsem.at[i])
        for i, (src, dst) in enumerate(
            ((wq_hbm, wq), (down_hbm, down), (kvw_hbm, kvw), (up_hbm, up))
        )
    ]
    for load in loads:
        load.start()
    rows, width = hidden.shape
    blocks[ring.me] = hidden[...]
    ring.barrier()

    def add_square(x):
        wide = x.astype(F32)
        total[...] += jnp.sum(wide * wide, axis=1, keepdims=True)

    def prepare(step):
        if step == 0:
            total[...] = jnp.zeros_like(total)
            add_square(hidden[...])
            query_sum[...] = jnp.zeros_like(query_sum)
            factor[...] = jnp.zeros_like(factor)

    query_sum = scatter[-1]
    scatter = scatter[:-1]
    gather_blocks(ring, blocks, gs, gr, prepare, lambda slot: add_square(blocks[slot]))
    inverse = lax.rsqrt(total[...] * (1.0 / (n * width)) + 1e-06)
    for load in loads:
        load.wait()

    def normalize(t, carry):
        part = columns(t, width)
        x = (blocks[t].astype(F32) * inverse * gain[:, part].astype(F32)).astype(BF16)
        normed[t] = x
        factor[...] += dot_t(down[:, part], x)
        return carry

    lax.fori_loop(0, n, normalize, 0)
    masked = jnp.where(ids[...] == ring.me, factor[...], 0.0).T.astype(BF16)
    own = normed[ring.me]
    devices_a_head = n // KVH

    def partial(chip, core):
        head = lax.div(chip * 2, devices_a_head)
        delta = dot(masked, up[:, columns(chip * 2 + core, width)])
        fresh = dot(own, kvw[:, columns(head * 2 + core, HD)])
        return jnp.concatenate([delta, fresh], axis=1)

    def project(t, carry):
        query_sum[...] += dot(normed[t], wq[columns(t, width), :])
        return carry

    def projects(step):
        part = share(step, ring.long, n)
        lax.fori_loop(part.start, part.stop, project, 0)

    value = scatter_sum(ring, partial, projects, *scatter)
    halves[ring.core] = value[:, width:].astype(BF16)
    swap = ring.copy(
        halves.at[ring.core], halves.at[ring.core], fsem.at[0], fsem.at[1], ring.mate
    )
    swap.start()
    query[...] = (query_sum[...] + adapter_scale * value[:, :width]).astype(BF16)
    swap.wait_send()
    other = halves.at[1 - ring.core]
    ring.copy(other, other, fsem.at[0], fsem.at[1], ring.mate).wait_recv()
    pair[...] = halves[...]


def second_kernel(
    n,
    attended,
    ids,
    wo_hbm,
    down_hbm,
    up_hbm,
    out,
    blocks,
    wo,
    down,
    up,
    base,
    factor,
    wsem,
    gs,
    gr,
    *scatter,
):
    ring = Ring(n)
    loads = [
        pltpu.make_async_copy(src, dst, wsem.at[i])
        for i, (src, dst) in enumerate(((down_hbm, down), (wo_hbm, wo), (up_hbm, up)))
    ]
    for load in loads:
        load.start()
    rows, width = attended.shape
    blocks[ring.me] = attended[...]
    ring.barrier()

    def on_block(slot):
        factor[...] += dot_t(down[:, columns(slot, width)], blocks[slot])

    def base_product(t, carry):
        base[t] = dot(attended[...], wo[:, columns(t, width)])
        return carry

    def fill(step):
        if step == 0:
            loads[0].wait()
            factor[...] = dot_t(down[:, columns(ring.me, width)], attended[...])
            return
        if step == 1:
            loads[1].wait()
            loads[2].wait()
        part = share(step - 1, ring.long, n)
        lax.fori_loop(part.start, part.stop, base_product, 0)

    gather_blocks(ring, blocks, gs, gr, fill, on_block)
    masked = jnp.where(ids[...] == ring.me, factor[...], 0.0).T.astype(BF16)

    def partial(chip, core):
        t = chip * 2 + core
        return base[t] + adapter_scale * dot(masked, up[:, columns(t, width)])

    out[...] = scatter_sum(ring, partial, lambda step: None, *scatter).astype(BF16)


VM = pl.BlockSpec(memory_space=pltpu.VMEM)
ANY = pl.BlockSpec(memory_space=pl.ANY)


def body(
    hidden_in,
    norm_gain,
    query_base_matrix,
    kv_weight,
    out_weight,
    query_down,
    query_up_factor,
    output_down,
    output_up_factor,
    variant_ids,
    cache_lengths,
    kv_cache,
):
    n = lax.axis_size("tensor")
    rows, width = hidden_in.shape
    depth = norm_gain.shape[0]
    rank = query_down.shape[2]
    params = functools.partial(
        pltpu.CompilerParams, has_side_effects=True, vmem_limit_bytes=VMEM_LIMIT
    )
    query_vectors, pair = pl.pallas_call(
        functools.partial(first_kernel, n),
        out_shape=[
            jax.ShapeDtypeStruct((rows, width), BF16),
            jax.ShapeDtypeStruct((2, rows, HD), BF16),
        ],
        in_specs=[VM] * 3 + [ANY] * 4,
        out_specs=[VM] * 2,
        scratch_shapes=[
            pltpu.VMEM((n, rows, width), BF16),
            pltpu.VMEM(query_base_matrix.shape, BF16),
            pltpu.VMEM(kv_weight.shape, BF16),
            pltpu.VMEM((rank, depth), BF16),
            pltpu.VMEM((rank, depth), BF16),
            pltpu.VMEM((n, rows, width), BF16),
            pltpu.VMEM((rows, 1), F32),
            pltpu.VMEM((rank, rows), F32),
            pltpu.VMEM((2, rows, HD), BF16),
            pltpu.SemaphoreType.DMA((4,)),
            *gather_sems(n),
            pltpu.SemaphoreType.DMA((2,)),
            *scatter_scratch(n, rows, width + HD),
            pltpu.VMEM((rows, width), F32),
        ],
        compiler_params=params(collective_id=0),
        name="gather_project",
    )(
        hidden_in,
        norm_gain[None],
        jnp.swapaxes(variant_ids, 0, 1),
        query_base_matrix,
        kv_weight,
        jnp.swapaxes(query_down, 1, 2)[0],
        query_up_factor[0],
    )
    fresh_key, fresh_value = pair[0], pair[1]
    local_heads = width // HD
    query_heads = query_vectors.reshape(rows, local_heads, HD)
    stored = kv_cache[0]
    keys = stored[:, :, :HD]
    values = stored[:, :, HD:]
    scale = 1.0 / HD**0.5
    scores = (
        jnp.einsum("rhd,rld->rhl", query_heads, keys, preferred_element_type=F32) * scale
    )
    own = jnp.einsum("rhd,rd->rh", query_heads, fresh_key, preferred_element_type=F32) * scale
    positions = jnp.arange(stored.shape[1], dtype=jnp.int32)
    live = positions[None, :] < cache_lengths[:, None]
    scores = jnp.where(live[:, None, :], scores, -jnp.inf)
    top = jnp.maximum(jnp.max(scores, axis=2), own)
    expo = jnp.exp(scores - top[:, :, None])
    own_expo = jnp.exp(own - top)
    total = jnp.sum(expo, axis=2) + own_expo
    weights = (expo / total[:, :, None]).astype(BF16)
    own_weight = (own_expo / total).astype(BF16)
    mixed_heads = jnp.einsum("rhl,rld->rhd", weights, values, preferred_element_type=F32)
    mixed_heads = (
        mixed_heads + own_weight.astype(F32)[:, :, None] * fresh_value.astype(F32)[:, None, :]
    )
    attended = mixed_heads.astype(BF16).reshape(rows, local_heads * HD)
    return pl.pallas_call(
        functools.partial(second_kernel, n),
        out_shape=jax.ShapeDtypeStruct((rows, width), BF16),
        in_specs=[VM] * 2 + [ANY] * 3,
        out_specs=VM,
        scratch_shapes=[
            pltpu.VMEM((n, rows, width), BF16),
            pltpu.VMEM(out_weight.shape, BF16),
            pltpu.VMEM((rank, depth), BF16),
            pltpu.VMEM((rank, depth), BF16),
            pltpu.VMEM((n, rows, width), F32),
            pltpu.VMEM((rank, rows), F32),
            pltpu.SemaphoreType.DMA((3,)),
            *gather_sems(n),
            *scatter_scratch(n, rows, width),
        ],
        compiler_params=params(collective_id=1),
        name="gather_output",
    )(
        attended,
        jnp.swapaxes(variant_ids, 0, 1),
        out_weight,
        jnp.swapaxes(output_down, 1, 2)[0],
        output_up_factor[0],
    )


def solution(mesh):
    in_specs = (
        P("groups", "tensor"),
        P(),
        P(None, "tensor"),
        P("tensor", None),
        P("tensor", None),
        P("tensor", None, None),
        P("tensor", None, None),
        P("tensor", None, None),
        P("tensor", None, None),
        P("groups", None),
        P("groups"),
        P("tensor", "groups", None, None),
    )
    out_specs = P("groups", "tensor")
    return jax.shard_map(body, mesh=mesh, in_specs=in_specs, out_specs=out_specs, check_vma=False)
```

```python
import functools

import jax
import jax.numpy as jnp
from jax import lax
from jax.experimental import pallas as pl
from jax.experimental.pallas import tpu as pltpu
from jax.sharding import PartitionSpec as P

H = 64
KVH = 8
HD = 128
MESH = pl.DeviceIdType.MESH
F32 = jnp.float32
BF16 = jnp.bfloat16
VMEM_LIMIT = 62 * 1024 * 1024

adapter_scale = 2.0


def chip_of(p, chips):
    if chips == 8:
        return 2 * p + lax.div(p, 4) * (15 - 4 * p)
    return p


def place_of(c, chips):
    if chips == 8:
        z = lax.div(c, 2)
        return z + lax.rem(c, 2) * (7 - 2 * z)
    return c


class Ring:
    def __init__(self, n):
        self.n = n
        self.chips = n // 2
        self.long = self.chips // 2
        self.short = self.chips - 1 - self.long
        self.me = lax.axis_index("tensor")
        self.core = lax.rem(self.me, 2)
        self.place = place_of(lax.div(self.me, 2), self.chips)
        self.sign = 1 - 2 * self.core
        self.right = self.at(1)
        self.left = self.at(-1)
        self.mate = self.chip(0) * 2 + 1 - self.core

    def chip(self, off):
        return chip_of(
            lax.rem(self.place + off * self.sign + 2 * self.chips, self.chips), self.chips
        )

    def at(self, off, other=False):
        core = 1 - self.core if other else self.core
        return self.chip(off) * 2 + core

    def barrier(self):
        sem = pltpu.get_barrier_semaphore()
        for device in (self.right, self.left, self.mate):
            pl.semaphore_signal(sem, inc=1, device_id={"tensor": device}, device_id_type=MESH)
        pl.semaphore_wait(sem, 3)

    def copy(self, src, dst, ssem, rsem, device):
        return pltpu.make_async_remote_copy(
            src_ref=src,
            dst_ref=dst,
            send_sem=ssem,
            recv_sem=rsem,
            device_id={"tensor": device},
            device_id_type=MESH,
        )


def gather_sems(n):
    return [pltpu.SemaphoreType.DMA((2, n - 1)), pltpu.SemaphoreType.DMA((2, n - 1))]


def half(ref, slot, h):
    rows = ref.shape[1] // 2
    return ref.at[slot, pl.ds(h * rows, rows)]


def gather_blocks(ring, blocks, ssem, rsem, filler, on_block):
    long, short, chips = ring.long, ring.short, ring.chips
    sent = []

    def copy(slot, h, index, device):
        ref = half(blocks, slot, h)
        return ring.copy(ref, ref, ssem.at[h, index], rsem.at[h, index], device)

    def send(slot, h, index, device):
        one = copy(slot, h, index, device)
        one.start()
        sent.append(one)

    hand = chips - 1
    for h in range(2):
        send(ring.me, h, 0, ring.right)
        send(ring.me, h, long, ring.left)
    for h in range(2):
        send(ring.me, h, hand, ring.mate)
    filler(0)

    def mates():
        for slot, index in waiting:
            for h in range(2):
                copy(slot, h, index, ring.mate).wait_recv()
            on_block(slot)

    waiting = [(ring.mate, hand)]
    ready = []
    for j in range(1, long + 1):
        slot, other = ring.at(-j), ring.at(j)
        for h in range(2):
            copy(slot, h, j - 1, ring.mate).wait_recv()
            if j < long:
                send(slot, h, j, ring.right)
            send(slot, h, hand + j, ring.mate)
            if j <= short:
                copy(other, h, long + j - 1, ring.mate).wait_recv()
                if j < short:
                    send(other, h, long + j, ring.left)
                send(other, h, hand + long + j, ring.mate)
            if h == 0:
                filler(2 * j - 1)
                for done in ready:
                    on_block(done)
            else:
                mates()
                filler(2 * j)
        ready = [slot]
        waiting = [(ring.at(j, True), hand + j)]
        if j <= short:
            ready.append(other)
            waiting.append((ring.at(-j, True), hand + long + j))
    for done in ready:
        on_block(done)
    mates()
    for one in sent:
        one.wait_send()


def scatter_scratch(n, rows, width):
    chips = n // 2
    return [
        pltpu.VMEM((chips, rows, width), BF16),
        pltpu.VMEM((chips, rows, width), BF16),
        pltpu.VMEM((chips - 1, rows, width), BF16),
        pltpu.VMEM((chips - 1, rows, width), BF16),
        pltpu.VMEM((2, rows, width), F32),
        pltpu.SemaphoreType.DMA((chips,)),
        pltpu.SemaphoreType.DMA((chips,)),
        pltpu.SemaphoreType.DMA((2, chips - 1)),
        pltpu.SemaphoreType.DMA((2, chips - 1)),
    ]


def scatter_sum(ring, partial, filler, hand_out, hand_in, going, coming, held, hs, hr, ssem, rsem):
    long, short, chips = ring.long, ring.short, ring.chips
    rows = going.shape[1] // 2
    steps = []
    for j in range(1, long + 1):
        now = [(2 * j - 2, long - j + 1, j - 1, ring.right, j == 1)]
        if j <= short:
            now.append((2 * j - 1, j - short - 1, long + j - 1, ring.left, j == 1))
        steps.append(now)
    sent = []

    def start(one):
        one.start()
        sent.append(one)

    def hand_copy(i):
        return ring.copy(hand_out.at[i], hand_in.at[i], hs.at[i], hr.at[i], ring.mate)

    def hand_over(i, o):
        hand_out[i] = partial(i, False, ring.chip(-o), 1 - ring.core).astype(BF16)
        start(hand_copy(i))

    def hand_overs(j):
        if j < long:
            for i, o, _, _, _ in steps[j]:
                hand_over(i, o)
        elif j == long:
            hand_over(chips - 1, 0)

    def both(i, o):
        value = partial(i, True, ring.chip(o), ring.core)
        ring.copy(hand_in.at[i], hand_in.at[i], hs.at[i], hr.at[i], ring.mate).wait_recv()
        return value + hand_in[i].astype(F32)

    def arrived(slot, h):
        ref = half(coming, slot, h)
        ring.copy(ref, ref, ssem.at[h, slot], rsem.at[h, slot], ring.mate).wait_recv()
        return ref[...].astype(F32)

    hand_overs(0)
    for j, now in enumerate(steps):
        for place, (i, o, slot, device, first) in enumerate(now):
            held[place] = both(i, o)
        for h in range(2):
            part = pl.ds(h * rows, rows)
            for place, (i, o, slot, device, first) in enumerate(now):
                value = held[place, part]
                if not first:
                    value = value + arrived(slot - 1, h)
                going[slot, part] = value.astype(BF16)
                start(
                    ring.copy(
                        half(going, slot, h),
                        half(coming, slot, h),
                        ssem.at[h, slot],
                        rsem.at[h, slot],
                        device,
                    )
                )
        if j == 0:
            hand_overs(1)
        hand_overs(j + 2)
        filler(j)
    held[0] = both(chips - 1, 0)
    for h in range(2):
        part = pl.ds(h * rows, rows)
        value = held[0, part] + arrived(long - 1, h)
        if short:
            value = value + arrived(long + short - 1, h)
        held[0, part] = value
    for one in sent:
        one.wait_send()
    return held[0]


def share(step, steps, count):
    return range(count * step // steps, count * (step + 1) // steps)


def columns(index, width):
    return pl.ds(pl.multiple_of(index * width, width), width)


def dot(a, b):
    return jnp.dot(a, b, preferred_element_type=F32)


def dot_t(a, b):
    return lax.dot_general(a, b, (((1,), (1,)), ((), ())), preferred_element_type=F32)


def first_kernel(
    n,
    hidden,
    gain,
    ids,
    wq_hbm,
    kvw_hbm,
    down_hbm,
    up_hbm,
    query,
    pair,
    blocks,
    wq,
    kvw,
    down,
    up,
    normed,
    total,
    factor,
    halves,
    wsem,
    gs,
    gr,
    fsem,
    *scatter,
):
    ring = Ring(n)
    loads = [
        pltpu.make_async_copy(src, dst, wsem.at[i])
        for i, (src, dst) in enumerate(
            ((wq_hbm, wq), (down_hbm, down), (kvw_hbm, kvw), (up_hbm, up))
        )
    ]
    for load in loads:
        load.start()
    rows, width = hidden.shape
    blocks[ring.me] = hidden[...]
    ring.barrier()

    def add_square(x):
        wide = x.astype(F32)
        total[...] += jnp.sum(wide * wide, axis=1, keepdims=True)

    def prepare(step):
        if step == 0:
            total[...] = jnp.zeros_like(total)
            add_square(hidden[...])
            query_sum[...] = jnp.zeros_like(query_sum)
            factor[...] = jnp.zeros_like(factor)

    query_sum = scatter[-1]
    scatter = scatter[:-1]
    gather_blocks(ring, blocks, gs, gr, prepare, lambda slot: add_square(blocks[slot]))
    inverse = lax.rsqrt(total[...] * (1.0 / (n * width)) + 1e-06)
    for load in loads:
        load.wait()

    def normalize(q, carry):
        terms = 0.0
        for t in (4 * q, 4 * q + 1, 4 * q + 2, 4 * q + 3):
            part = columns(t, width)
            scale = gain[part].astype(F32)[None, :] if len(gain.shape) == 1 else gain[:, part]
            x = (blocks[t].astype(F32) * inverse * scale.astype(F32)).astype(BF16)
            normed[t] = x
            terms = terms + dot_t(down[:, part], x)
        factor[...] += terms
        return carry

    lax.fori_loop(0, n // 4, normalize, 0)
    masked = jnp.where(ids[...] == ring.me, factor[...], 0.0).T.astype(BF16)
    own = normed[ring.me]
    devices_a_head = n // KVH

    def partial(i, mine, chip, core):
        head = lax.div(chip * 2, devices_a_head)
        delta = dot(masked, up[:, columns(chip * 2 + core, width)])
        fresh = dot(own, kvw[:, columns(head * 2 + core, HD)])
        return jnp.concatenate([delta, fresh], axis=1)

    def project(t, carry):
        query_sum[...] += dot(normed[t], wq[columns(t, width), :])
        return carry

    def projects(step):
        part = share(step, ring.long, n)
        lax.fori_loop(part.start, part.stop, project, 0)

    value = scatter_sum(ring, partial, projects, *scatter)
    halves[ring.core] = value[:, width:].astype(BF16)
    swap = ring.copy(
        halves.at[ring.core], halves.at[ring.core], fsem.at[0], fsem.at[1], ring.mate
    )
    swap.start()
    query[...] = (query_sum[...] + adapter_scale * value[:, :width]).astype(BF16)
    swap.wait_send()
    other = halves.at[1 - ring.core]
    ring.copy(other, other, fsem.at[0], fsem.at[1], ring.mate).wait_recv()
    pair[...] = halves[...]


def second_kernel(
    n,
    attended,
    ids,
    wo_hbm,
    down_hbm,
    up_hbm,
    out,
    blocks,
    wo,
    down,
    up,
    base,
    factor,
    wsem,
    gs,
    gr,
    *scatter,
):
    ring = Ring(n)
    loads = [
        pltpu.make_async_copy(src, dst, wsem.at[i])
        for i, (src, dst) in enumerate(((down_hbm, down), (wo_hbm, wo), (up_hbm, up)))
    ]
    for load in loads:
        load.start()
    rows, width = attended.shape
    blocks[ring.me] = attended[...]
    ring.barrier()

    def on_block(slot):
        factor[...] += dot_t(down[:, columns(slot, width)], blocks[slot])

    def base_product(chip, core):
        return dot(attended[...], wo[:, columns(chip * 2 + core, width)])

    ahead = base.shape[0] // 2

    def fill(step):
        if step == 0:
            loads[0].wait()
            factor[...] = dot_t(down[:, columns(ring.me, width)], attended[...])
            return
        if step == 1:
            loads[1].wait()
        for item in share(step - 1, 2 * ring.long, 2 * ahead):
            i, mine = item // 2, item % 2
            o = ring.long - i // 2 if i % 2 == 0 else i // 2 - ring.short
            if mine:
                base[item] = base_product(ring.chip(o), ring.core)
            else:
                base[item] = base_product(ring.chip(-o), 1 - ring.core)

    gather_blocks(ring, blocks, gs, gr, fill, on_block)
    loads[2].wait()
    masked = jnp.where(ids[...] == ring.me, factor[...], 0.0).T.astype(BF16)

    def partial(i, mine, chip, core):
        if i < ahead:
            first = base[2 * i + 1] if mine else base[2 * i]
        else:
            first = base_product(chip, core)
        return first + adapter_scale * dot(masked, up[:, columns(chip * 2 + core, width)])

    out[...] = scatter_sum(ring, partial, lambda step: None, *scatter).astype(BF16)


VM = pl.BlockSpec(memory_space=pltpu.VMEM)
ANY = pl.BlockSpec(memory_space=pl.ANY)


def body(
    hidden_in,
    norm_gain,
    query_base_matrix,
    kv_weight,
    out_weight,
    query_down,
    query_up_factor,
    output_down,
    output_up_factor,
    variant_ids,
    cache_lengths,
    kv_cache,
):
    n = lax.axis_size("tensor")
    rows, width = hidden_in.shape
    depth = norm_gain.shape[0]
    rank = query_down.shape[2]
    params = functools.partial(
        pltpu.CompilerParams, has_side_effects=True, vmem_limit_bytes=VMEM_LIMIT
    )
    query_vectors, pair = pl.pallas_call(
        functools.partial(first_kernel, n),
        out_shape=[
            jax.ShapeDtypeStruct((rows, width), BF16),
            jax.ShapeDtypeStruct((2, rows, HD), BF16),
        ],
        in_specs=[VM] * 3 + [ANY] * 4,
        out_specs=[VM] * 2,
        scratch_shapes=[
            pltpu.VMEM((n, rows, width), BF16),
            pltpu.VMEM(query_base_matrix.shape, BF16),
            pltpu.VMEM(kv_weight.shape, BF16),
            pltpu.VMEM((rank, depth), BF16),
            pltpu.VMEM((rank, depth), BF16),
            pltpu.VMEM((n, rows, width), BF16),
            pltpu.VMEM((rows, 1), F32),
            pltpu.VMEM((rank, rows), F32),
            pltpu.VMEM((2, rows, HD), BF16),
            pltpu.SemaphoreType.DMA((4,)),
            *gather_sems(n),
            pltpu.SemaphoreType.DMA((2,)),
            *scatter_scratch(n, rows, width + HD),
            pltpu.VMEM((rows, width), F32),
        ],
        compiler_params=params(collective_id=0),
        name="gather_project",
    )(
        hidden_in,
        norm_gain if width % 512 == 0 else norm_gain[None],
        jnp.swapaxes(variant_ids, 0, 1),
        query_base_matrix,
        kv_weight,
        jnp.swapaxes(query_down, 1, 2)[0],
        query_up_factor[0],
    )
    fresh_key, fresh_value = pair[0], pair[1]
    local_heads = width // HD
    query_heads = query_vectors.reshape(rows, local_heads, HD)
    stored = kv_cache[0]
    keys = stored[:, :, :HD]
    values = stored[:, :, HD:]
    scale = 1.0 / HD**0.5
    scores = (
        jnp.einsum("rhd,rld->rhl", query_heads, keys, preferred_element_type=F32) * scale
    )
    own = jnp.einsum("rhd,rd->rh", query_heads, fresh_key, preferred_element_type=F32) * scale
    positions = jnp.arange(stored.shape[1], dtype=jnp.int32)
    live = positions[None, :] < cache_lengths[:, None]
    scores = jnp.where(live[:, None, :], scores, -jnp.inf)
    top = jnp.maximum(jnp.max(scores, axis=2), own)
    expo = jnp.exp(scores - top[:, :, None])
    own_expo = jnp.exp(own - top)
    total = jnp.sum(expo, axis=2) + own_expo
    weights = (expo / total[:, :, None]).astype(BF16)
    own_weight = (own_expo / total).astype(BF16)
    mixed_heads = jnp.einsum("rhl,rld->rhd", weights, values, preferred_element_type=F32)
    mixed_heads = (
        mixed_heads + own_weight.astype(F32)[:, :, None] * fresh_value.astype(F32)[:, None, :]
    )
    attended = mixed_heads.astype(BF16).reshape(rows, local_heads * HD)
    return pl.pallas_call(
        functools.partial(second_kernel, n),
        out_shape=jax.ShapeDtypeStruct((rows, width), BF16),
        in_specs=[VM] * 2 + [ANY] * 3,
        out_specs=VM,
        scratch_shapes=[
            pltpu.VMEM((n, rows, width), BF16),
            pltpu.VMEM(out_weight.shape, BF16),
            pltpu.VMEM((rank, depth), BF16),
            pltpu.VMEM((rank, depth), BF16),
            pltpu.VMEM((8, rows, width), F32),
            pltpu.VMEM((rank, rows), F32),
            pltpu.SemaphoreType.DMA((3,)),
            *gather_sems(n),
            *scatter_scratch(n, rows, width),
        ],
        compiler_params=params(collective_id=1),
        name="gather_output",
    )(
        attended,
        jnp.swapaxes(variant_ids, 0, 1),
        out_weight,
        jnp.swapaxes(output_down, 1, 2)[0],
        output_up_factor[0],
    )


def solution(mesh):
    in_specs = (
        P("groups", "tensor"),
        P(),
        P(None, "tensor"),
        P("tensor", None),
        P("tensor", None),
        P("tensor", None, None),
        P("tensor", None, None),
        P("tensor", None, None),
        P("tensor", None, None),
        P("groups", None),
        P("groups"),
        P("tensor", "groups", None, None),
    )
    out_specs = P("groups", "tensor")
    return jax.shard_map(body, mesh=mesh, in_specs=in_specs, out_specs=out_specs, check_vma=False)
```

```python
import functools

import jax
import jax.numpy as jnp
from jax import lax
from jax.experimental import pallas as pl
from jax.experimental.pallas import tpu as pltpu
from jax.sharding import PartitionSpec as P

H = 64
KVH = 8
HD = 128
MESH = pl.DeviceIdType.MESH
F32 = jnp.float32
BF16 = jnp.bfloat16
VMEM_LIMIT = 62 * 1024 * 1024

adapter_scale = 2.0


def chip_of(p, chips):
    if chips == 8:
        return 2 * p + lax.div(p, 4) * (15 - 4 * p)
    return p


def place_of(c, chips):
    if chips == 8:
        z = lax.div(c, 2)
        return z + lax.rem(c, 2) * (7 - 2 * z)
    return c


class Ring:
    def __init__(self, n):
        self.n = n
        self.chips = n // 2
        self.long = self.chips // 2
        self.short = self.chips - 1 - self.long
        self.me = lax.axis_index("tensor")
        self.core = lax.rem(self.me, 2)
        self.place = place_of(lax.div(self.me, 2), self.chips)
        self.sign = 1 - 2 * self.core
        self.right = self.at(1)
        self.left = self.at(-1)
        self.mate = self.chip(0) * 2 + 1 - self.core

    def chip(self, off):
        return chip_of(
            lax.rem(self.place + off * self.sign + 2 * self.chips, self.chips), self.chips
        )

    def at(self, off, other=False):
        core = 1 - self.core if other else self.core
        return self.chip(off) * 2 + core

    def barrier(self):
        sem = pltpu.get_barrier_semaphore()
        for device in (self.right, self.left, self.mate):
            pl.semaphore_signal(sem, inc=1, device_id={"tensor": device}, device_id_type=MESH)
        pl.semaphore_wait(sem, 3)

    def copy(self, src, dst, ssem, rsem, device):
        return pltpu.make_async_remote_copy(
            src_ref=src,
            dst_ref=dst,
            send_sem=ssem,
            recv_sem=rsem,
            device_id={"tensor": device},
            device_id_type=MESH,
        )


def gather_sems(n):
    return [pltpu.SemaphoreType.DMA((2, n - 1)), pltpu.SemaphoreType.DMA((2, n - 1))]


def half(ref, slot, h):
    rows = ref.shape[1] // 2
    return ref.at[slot, pl.ds(h * rows, rows)]


def gather_blocks(ring, blocks, ssem, rsem, filler, on_block):
    long, short, chips = ring.long, ring.short, ring.chips
    sent = []

    def copy(slot, h, index, device):
        ref = half(blocks, slot, h)
        return ring.copy(ref, ref, ssem.at[h, index], rsem.at[h, index], device)

    def send(slot, h, index, device):
        one = copy(slot, h, index, device)
        one.start()
        sent.append(one)

    hand = chips - 1
    for h in range(2):
        send(ring.me, h, 0, ring.right)
        send(ring.me, h, long, ring.left)
    for h in range(2):
        send(ring.me, h, hand, ring.mate)
    filler(0)

    def mates():
        for slot, index in waiting:
            for h in range(2):
                copy(slot, h, index, ring.mate).wait_recv()
            on_block(slot)

    waiting = [(ring.mate, hand)]
    ready = []
    for j in range(1, long + 1):
        slot, other = ring.at(-j), ring.at(j)
        for h in range(2):
            copy(slot, h, j - 1, ring.mate).wait_recv()
            if j < long:
                send(slot, h, j, ring.right)
            send(slot, h, hand + j, ring.mate)
            if j <= short:
                copy(other, h, long + j - 1, ring.mate).wait_recv()
                if j < short:
                    send(other, h, long + j, ring.left)
                send(other, h, hand + long + j, ring.mate)
            if h == 0:
                filler(2 * j - 1)
                for done in ready:
                    on_block(done)
            else:
                mates()
                filler(2 * j)
        ready = [slot]
        waiting = [(ring.at(j, True), hand + j)]
        if j <= short:
            ready.append(other)
            waiting.append((ring.at(-j, True), hand + long + j))
    for done in ready:
        on_block(done)
    mates()
    for one in sent:
        one.wait_send()


def scatter_scratch(n, rows, width):
    chips = n // 2
    return [
        pltpu.VMEM((chips, rows, width), BF16),
        pltpu.VMEM((chips, rows, width), BF16),
        pltpu.VMEM((chips - 1, rows, width), BF16),
        pltpu.VMEM((chips - 1, rows, width), BF16),
        pltpu.VMEM((2, rows, width), F32),
        pltpu.SemaphoreType.DMA((chips,)),
        pltpu.SemaphoreType.DMA((chips,)),
        pltpu.SemaphoreType.DMA((2, chips - 1)),
        pltpu.SemaphoreType.DMA((2, chips - 1)),
    ]


def scatter_sum(ring, partial, filler, hand_out, hand_in, going, coming, held, hs, hr, ssem, rsem):
    long, short, chips = ring.long, ring.short, ring.chips
    rows = going.shape[1] // 2
    steps = []
    for j in range(1, long + 1):
        now = [(2 * j - 2, long - j + 1, j - 1, ring.right, j == 1)]
        if j <= short:
            now.append((2 * j - 1, j - short - 1, long + j - 1, ring.left, j == 1))
        steps.append(now)
    sent = []

    def start(one):
        one.start()
        sent.append(one)

    def hand_copy(i):
        return ring.copy(hand_out.at[i], hand_in.at[i], hs.at[i], hr.at[i], ring.mate)

    def hand_over(i, o):
        hand_out[i] = partial(i, False, ring.chip(-o), 1 - ring.core).astype(BF16)
        start(hand_copy(i))

    def hand_overs(j):
        if j < long:
            for i, o, _, _, _ in steps[j]:
                hand_over(i, o)
        elif j == long:
            hand_over(chips - 1, 0)

    def both(i, o):
        value = partial(i, True, ring.chip(o), ring.core)
        ring.copy(hand_in.at[i], hand_in.at[i], hs.at[i], hr.at[i], ring.mate).wait_recv()
        return value + hand_in[i].astype(F32)

    def arrived(slot, h):
        ref = half(coming, slot, h)
        ring.copy(ref, ref, ssem.at[h, slot], rsem.at[h, slot], ring.mate).wait_recv()
        return ref[...].astype(F32)

    hand_overs(0)
    for j, now in enumerate(steps):
        for place, (i, o, slot, device, first) in enumerate(now):
            held[place] = both(i, o)
        for h in range(2):
            part = pl.ds(h * rows, rows)
            for place, (i, o, slot, device, first) in enumerate(now):
                value = held[place, part]
                if not first:
                    value = value + arrived(slot - 1, h)
                going[slot, part] = value.astype(BF16)
                start(
                    ring.copy(
                        half(going, slot, h),
                        half(coming, slot, h),
                        ssem.at[h, slot],
                        rsem.at[h, slot],
                        device,
                    )
                )
        if j == 0:
            hand_overs(1)
        hand_overs(j + 2)
        filler(j)
    held[0] = both(chips - 1, 0)
    for h in range(2):
        part = pl.ds(h * rows, rows)
        value = held[0, part] + arrived(long - 1, h)
        if short:
            value = value + arrived(long + short - 1, h)
        held[0, part] = value
    for one in sent:
        one.wait_send()
    return held[0]


def share(step, steps, count):
    return range(count * step // steps, count * (step + 1) // steps)


def columns(index, width):
    return pl.ds(pl.multiple_of(index * width, width), width)


def dot(a, b):
    return jnp.dot(a, b, preferred_element_type=F32)


def dot_t(a, b):
    return lax.dot_general(a, b, (((1,), (1,)), ((), ())), preferred_element_type=F32)


def first_kernel(
    n,
    hidden,
    gain,
    ids,
    wq_hbm,
    kvw_hbm,
    down_hbm,
    up_hbm,
    query,
    own_score,
    fresh_value,
    blocks,
    wq,
    kvw,
    down,
    up,
    normed,
    total,
    factor,
    halves,
    wsem,
    gs,
    gr,
    fsem,
    *scatter,
):
    ring = Ring(n)
    loads = [
        pltpu.make_async_copy(src, dst, wsem.at[i])
        for i, (src, dst) in enumerate(
            ((wq_hbm, wq), (down_hbm, down), (kvw_hbm, kvw), (up_hbm, up))
        )
    ]
    for load in loads:
        load.start()
    rows, width = hidden.shape
    blocks[ring.me] = hidden[...]
    ring.barrier()

    def add_square(x):
        wide = x.astype(F32)
        total[...] += jnp.sum(wide * wide, axis=1, keepdims=True)

    def prepare(step):
        if step == 0:
            total[...] = jnp.zeros_like(total)
            add_square(hidden[...])
            query_sum[...] = jnp.zeros_like(query_sum)
            factor[...] = jnp.zeros_like(factor)

    query_sum = scatter[-1]
    scatter = scatter[:-1]
    gather_blocks(ring, blocks, gs, gr, prepare, lambda slot: add_square(blocks[slot]))
    inverse = lax.rsqrt(total[...] * (1.0 / (n * width)) + 1e-06)
    for load in loads:
        load.wait()

    def normalize(q, carry):
        terms = 0.0
        for t in (4 * q, 4 * q + 1, 4 * q + 2, 4 * q + 3):
            part = columns(t, width)
            scale = gain[part].astype(F32)[None, :] if len(gain.shape) == 1 else gain[:, part]
            x = (blocks[t].astype(F32) * inverse * scale.astype(F32)).astype(BF16)
            normed[t] = x
            terms = terms + dot_t(down[:, part], x)
        factor[...] += terms
        return carry

    lax.fori_loop(0, n // 4, normalize, 0)
    masked = jnp.where(ids[...] == ring.me, factor[...], 0.0).T.astype(BF16)
    own = normed[ring.me]
    devices_a_head = n // KVH

    def partial(i, mine, chip, core):
        head = lax.div(chip * 2, devices_a_head)
        delta = dot(masked, up[:, columns(chip * 2 + core, width)])
        fresh = dot(own, kvw[:, columns(head * 2 + core, HD)])
        return jnp.concatenate([delta, fresh], axis=1)

    def project(t, carry):
        query_sum[...] += dot(normed[t], wq[columns(t, width), :])
        return carry

    def projects(step):
        part = share(step, ring.long, n)
        lax.fori_loop(part.start, part.stop, project, 0)

    value = scatter_sum(ring, partial, projects, *scatter)
    halves[ring.core] = value[:, width:].astype(BF16)
    swap = ring.copy(
        halves.at[ring.core], halves.at[ring.core], fsem.at[0], fsem.at[1], ring.mate
    )
    swap.start()
    final = (query_sum[...] + adapter_scale * value[:, :width]).astype(BF16)
    query[...] = final
    swap.wait_send()
    other = halves.at[1 - ring.core]
    ring.copy(other, other, fsem.at[0], fsem.at[1], ring.mate).wait_recv()
    fresh_value[...] = halves[1]
    key = halves[0].astype(F32)
    for h in range(width // HD):
        head = final[:, h * HD : (h + 1) * HD].astype(F32)
        own_score[:, h : h + 1] = jnp.sum(head * key, axis=1, keepdims=True) * (1.0 / HD**0.5)


def second_kernel(
    n,
    attended,
    ids,
    wo_hbm,
    down_hbm,
    up_hbm,
    out,
    blocks,
    wo,
    down,
    up,
    base,
    factor,
    wsem,
    gs,
    gr,
    *scatter,
):
    ring = Ring(n)
    loads = [
        pltpu.make_async_copy(src, dst, wsem.at[i])
        for i, (src, dst) in enumerate(((down_hbm, down), (wo_hbm, wo), (up_hbm, up)))
    ]
    for load in loads:
        load.start()
    rows, width = attended.shape
    blocks[ring.me] = attended[...]
    ring.barrier()

    def on_block(slot):
        factor[...] += dot_t(down[:, columns(slot, width)], blocks[slot])

    def base_product(chip, core):
        return dot(attended[...], wo[:, columns(chip * 2 + core, width)])

    ahead = base.shape[0] // 2

    def fill(step):
        if step == 0:
            loads[0].wait()
            factor[...] = dot_t(down[:, columns(ring.me, width)], attended[...])
            return
        if step == 1:
            loads[1].wait()
        for item in share(step - 1, 2 * ring.long, 2 * ahead):
            i, mine = item // 2, item % 2
            o = ring.long - i // 2 if i % 2 == 0 else i // 2 - ring.short
            if mine:
                base[item] = base_product(ring.chip(o), ring.core)
            else:
                base[item] = base_product(ring.chip(-o), 1 - ring.core)

    gather_blocks(ring, blocks, gs, gr, fill, on_block)
    loads[2].wait()
    masked = jnp.where(ids[...] == ring.me, factor[...], 0.0).T.astype(BF16)

    def partial(i, mine, chip, core):
        if i < ahead:
            first = base[2 * i + 1] if mine else base[2 * i]
        else:
            first = base_product(chip, core)
        return first + adapter_scale * dot(masked, up[:, columns(chip * 2 + core, width)])

    out[...] = scatter_sum(ring, partial, lambda step: None, *scatter).astype(BF16)


VM = pl.BlockSpec(memory_space=pltpu.VMEM)
ANY = pl.BlockSpec(memory_space=pl.ANY)


def body(
    hidden_in,
    norm_gain,
    query_base_matrix,
    kv_weight,
    out_weight,
    query_down,
    query_up_factor,
    output_down,
    output_up_factor,
    variant_ids,
    cache_lengths,
    kv_cache,
):
    n = lax.axis_size("tensor")
    rows, width = hidden_in.shape
    depth = norm_gain.shape[0]
    rank = query_down.shape[2]
    params = functools.partial(
        pltpu.CompilerParams, has_side_effects=True, vmem_limit_bytes=VMEM_LIMIT
    )
    query_vectors, own, fresh_value = pl.pallas_call(
        functools.partial(first_kernel, n),
        out_shape=[
            jax.ShapeDtypeStruct((rows, width), BF16),
            jax.ShapeDtypeStruct((rows, width // HD), F32),
            jax.ShapeDtypeStruct((rows, HD), BF16),
        ],
        in_specs=[VM] * 3 + [ANY] * 4,
        out_specs=[VM] * 3,
        scratch_shapes=[
            pltpu.VMEM((n, rows, width), BF16),
            pltpu.VMEM(query_base_matrix.shape, BF16),
            pltpu.VMEM(kv_weight.shape, BF16),
            pltpu.VMEM((rank, depth), BF16),
            pltpu.VMEM((rank, depth), BF16),
            pltpu.VMEM((n, rows, width), BF16),
            pltpu.VMEM((rows, 1), F32),
            pltpu.VMEM((rank, rows), F32),
            pltpu.VMEM((2, rows, HD), BF16),
            pltpu.SemaphoreType.DMA((4,)),
            *gather_sems(n),
            pltpu.SemaphoreType.DMA((2,)),
            *scatter_scratch(n, rows, width + HD),
            pltpu.VMEM((rows, width), F32),
        ],
        compiler_params=params(collective_id=0),
        name="gather_project",
    )(
        hidden_in,
        norm_gain if width % 512 == 0 else norm_gain[None],
        jnp.swapaxes(variant_ids, 0, 1),
        query_base_matrix,
        kv_weight,
        jnp.swapaxes(query_down, 1, 2)[0],
        query_up_factor[0],
    )
    local_heads = width // HD
    query_heads = query_vectors.reshape(rows, local_heads, HD)
    stored = kv_cache[0]
    keys = stored[:, :, :HD]
    values = stored[:, :, HD:]
    scale = 1.0 / HD**0.5
    scores = (
        jnp.einsum("rhd,rld->rhl", query_heads, keys, preferred_element_type=F32) * scale
    )
    positions = jnp.arange(stored.shape[1], dtype=jnp.int32)
    live = positions[None, :] < cache_lengths[:, None]
    scores = jnp.where(live[:, None, :], scores, -jnp.inf)
    top = jnp.maximum(jnp.max(scores, axis=2), own)
    expo = jnp.exp(scores - top[:, :, None])
    own_expo = jnp.exp(own - top)
    total = jnp.sum(expo, axis=2) + own_expo
    weights = (expo / total[:, :, None]).astype(BF16)
    own_weight = (own_expo / total).astype(BF16)
    mixed_heads = jnp.einsum("rhl,rld->rhd", weights, values, preferred_element_type=F32)
    mixed_heads = (
        mixed_heads + own_weight.astype(F32)[:, :, None] * fresh_value.astype(F32)[:, None, :]
    )
    attended = mixed_heads.astype(BF16).reshape(rows, local_heads * HD)
    return pl.pallas_call(
        functools.partial(second_kernel, n),
        out_shape=jax.ShapeDtypeStruct((rows, width), BF16),
        in_specs=[VM] * 2 + [ANY] * 3,
        out_specs=VM,
        scratch_shapes=[
            pltpu.VMEM((n, rows, width), BF16),
            pltpu.VMEM(out_weight.shape, BF16),
            pltpu.VMEM((rank, depth), BF16),
            pltpu.VMEM((rank, depth), BF16),
            pltpu.VMEM((8, rows, width), F32),
            pltpu.VMEM((rank, rows), F32),
            pltpu.SemaphoreType.DMA((3,)),
            *gather_sems(n),
            *scatter_scratch(n, rows, width),
        ],
        compiler_params=params(collective_id=1),
        name="gather_output",
    )(
        attended,
        jnp.swapaxes(variant_ids, 0, 1),
        out_weight,
        jnp.swapaxes(output_down, 1, 2)[0],
        output_up_factor[0],
    )


def solution(mesh):
    in_specs = (
        P("groups", "tensor"),
        P(),
        P(None, "tensor"),
        P("tensor", None),
        P("tensor", None),
        P("tensor", None, None),
        P("tensor", None, None),
        P("tensor", None, None),
        P("tensor", None, None),
        P("groups", None),
        P("groups"),
        P("tensor", "groups", None, None),
    )
    out_specs = P("groups", "tensor")
    return jax.shard_map(body, mesh=mesh, in_specs=in_specs, out_specs=out_specs, check_vma=False)
```
